32 devices in a mesh: groups: 2 (over y), expert: 8 (over z, core), tensor: 1, side: 2 (over x).
Axes of the slice: x: 2, y: 2, z: 4, core: 2. Of those that a mesh axis runs over, the one named last changes fastest.
Arguments:
- queries: bfloat16 [128, 64, 576], P(('groups', 'expert')), parts along dimension 0, may hold values from -30 to 30
- latent_cache: bfloat16 [128, 1024, 576], P(('groups', 'expert'), ('tensor', 'side')), parts along dimension 0, may hold values from -5 to 5
- lengths: int32 [128], P(('groups', 'expert')), parts along dimension 0, may hold values from 2 to 1024, as said below
- assignment: int32 [128], P('groups'), parts along dimension 0, may hold values from 0 to 63, each once
- w_uv: bfloat16 [64, 512, 128], P(('tensor', 'side')), may hold values from -0.25 to 0.25
- w_o: bfloat16 [8192, 3584], P(('tensor', 'side'), 'expert'), may hold values from -0.26367188 to 0.26367188
- residual: bfloat16 [128, 3584], P('groups', 'expert'), parts along dimension 0, may hold values from -3 to 3
- gain: bfloat16 [3584], P('expert'), may hold values from 0.099609375 to 1.8984375
- expert_ids: int32 [128, 8], P('groups'), parts along dimension 0, may hold values from 0 to 15, all different within a row; in each aligned block of 64 rows (0 to 63, 64 to 127, ...) at most 64 rows name the same one
- expert_weights: float32 [128, 8], P('groups'), parts along dimension 0, may hold values from 0.1 to 1
- w_gate: bfloat16 [16, 3584, 1024], P(('expert', 'side'), None, 'tensor'), may hold values from -0.09375 to 0.09375
- w_up: bfloat16 [16, 3584, 1024], P(('expert', 'side'), None, 'tensor'), may hold values from -0.09375 to 0.09375
- w_down: bfloat16 [16, 1024, 3584], P(('expert', 'side'), 'tensor'), may hold values from -0.1875 to 0.1875
Outputs:
- layer_out: float32 [128, 3584], P('groups', 'expert'), parts along dimension 0
The draws below stay inside these ranges and needn't reach their ends.
There are 2 independent parts, one for each index of `groups`. The reference program is written for one: setup_inputs(seed, part) draws one part's arguments, and reference() takes and returns one part's arrays. A program takes and returns all parts, laid end to end along the dimension named above; an argument that names none is the same for every part. Nothing has to cross between parts.
Inputs may be any that keep to these rules, and one draw needn't show every extreme that they name: `lengths`: each request's cache is filled at positions below its length; some request has exactly 1024. `expert_ids`: no expert is chosen by more than 64 tokens, and some expert is chosen by exactly 64.
All inputs are finite; a program needn't handle non-finite values.
Results may differ from the reference program's by a relative error of at most 0.0037.
The reference program's roundings to bfloat16 on the way count: a program that leaves them out, or rounds other values in their place, can miss the bound.
Values may be sent and summed in bfloat16 or wider, within the bound.
A program may use at most 128 MiB of HBM per device.

```python
import math
import jax
import jax.numpy as jnp
import numpy as np
from jax import lax

D = 3584
FF = 1024
HEADS = 64
KV_LAT = 512
ROPE = 64
V_HEAD = 128
TOP = 8
LMAX = 1024
TOKEN_TOTAL = 64
EXPERTS = 16
CAP = 64


score_scale = 0.07216878364870323


def aimed_parts(key, gauss_share, spread, low_target, upper_goal, share):
    width = KV_LAT + ROPE
    size_part = jax.random.uniform(jax.random.fold_in(key, 12), (TOKEN_TOTAL, width), jnp.float32, minval=3.0, maxval=5.0)
    sign_part = jnp.where(jax.random.uniform(jax.random.fold_in(key, 13), (TOKEN_TOTAL, width)) < 0.5, -1.0, 1.0)
    normal_part = jnp.clip(jax.random.normal(jax.random.fold_in(key, 19), (TOKEN_TOTAL, width), jnp.float32), -3.0, 3.0)
    aimed = gauss_share * normal_part + (1.0 - gauss_share) * size_part * sign_part
    place = jax.random.randint(jax.random.fold_in(key, 14), (TOKEN_TOTAL,), 0, spread, jnp.int32)
    target = jax.random.uniform(jax.random.fold_in(key, 15), (TOKEN_TOTAL,), jnp.float32, minval=low_target, maxval=upper_goal)
    delta = jax.random.uniform(jax.random.fold_in(key, 16), (TOKEN_TOTAL,), jnp.float32, minval=1.0, maxval=3.0)
    turn_sign = jnp.where(jax.random.uniform(jax.random.fold_in(key, 20), (TOKEN_TOTAL,)) < 0.5, -1.0, 1.0)
    turn = turn_sign * jax.random.uniform(jax.random.fold_in(key, 17), (TOKEN_TOTAL,), jnp.float32, minval=0.4, maxval=0.6)
    chosen = jax.random.uniform(jax.random.fold_in(key, 18), (TOKEN_TOTAL,)) < share
    return (aimed, place, target, delta, turn, chosen)


def draw_latent_cache(key, part):
    aimed, place, target, delta, turn, chosen = aimed_parts(key, 0.0, 1, 110.0, 200.0, 0.25)
    key = jax.random.fold_in(key, 3)
    cache = jnp.clip(jax.random.normal(key, (TOKEN_TOTAL, LMAX, KV_LAT + ROPE), jnp.float32), -5.0, 5.0)
    row_index = jnp.arange(TOKEN_TOTAL, dtype=jnp.int32)
    cache = cache.at[row_index, place, :].set(aimed)
    return cache.astype(jnp.bfloat16)


def draw_queries(key, part):
    aimed, place, target, delta, turn, chosen = aimed_parts(key, 0.0, 1, 110.0, 200.0, 0.25)
    key_energy = jnp.sum(aimed * aimed, axis=1)
    key = jax.random.fold_in(key, 5)
    sampled_values = jnp.clip(jax.random.normal(key, (TOKEN_TOTAL, HEADS, KV_LAT + ROPE), jnp.float32), -5.0, 5.0)
    strength = target / (score_scale * key_energy)
    pointed = jnp.clip(strength[:, None] * aimed, -30.0, 30.0)
    sampled_values = jnp.where(chosen[:, None, None], pointed[:, None, :], sampled_values)
    return sampled_values.astype(jnp.bfloat16)


def draw_lengths(key, part):
    key = jax.random.fold_in(key, 9)
    sampled_values = jax.random.randint(key, (TOKEN_TOTAL,), 2, LMAX + 1, jnp.int32)
    longest = jax.random.randint(jax.random.fold_in(key, 10), (), 0, TOKEN_TOTAL, jnp.int32)
    return sampled_values.at[longest].set(LMAX)


def draw_expert_weights(key, part):
    key = jax.random.fold_in(key, 21)
    sampled_values = jnp.exp(jax.random.uniform(key, (TOKEN_TOTAL, TOP), jnp.float32, minval=math.log(0.1), maxval=0.0))
    return jnp.clip(sampled_values, 0.1, 1.0)


def level_of(own_key, extent, pieces, low, largest):
    level = 1.0
    for position, shards_of in pieces:
        steps = jax.random.uniform(jax.random.fold_in(jax.random.fold_in(own_key, 6), position), (shards_of,), jnp.float32, low / len(pieces), largest / len(pieces))
        level = level * jnp.repeat(jnp.exp(steps), extent[position] // shards_of).reshape((-1,) + (1,) * (len(extent) - 1 - position))
    return level


def shared_out(rng, own, number, rows, amount, top, limit, skew):
    order = jax.random.permutation(rng, amount)
    crowded, ordinary = portions_of(amount, rows * top, limit, skew, True), portions_of(amount, rows * top, limit, skew, False)
    places = jnp.arange(amount)

    def named(sizes, rotation):
        used = int((sizes > 0).sum())
        fixed = max(1, used // 4)
        shifted = fixed + (places - fixed + rotation * (used - fixed)) % max(1, amount - fixed)
        return jnp.zeros((amount,), jnp.int32).at[order[jnp.where(places < fixed, places, shifted)]].set(jnp.asarray(sizes, jnp.int32))

    sizes = jnp.where(number % 4 == 0, named(crowded, number // 4), named(ordinary, number - number // 4 - 1))
    mixed = jax.random.permutation(jax.random.fold_in(own, 3), amount)
    source_of, sink = mixed[0:amount // 2 * 2:2], mixed[1:amount // 2 * 2:2]
    slack = jnp.minimum(sizes[source_of] - 1, limit - sizes[sink]) // 2
    slack = jnp.where((source_of == order[0]) | (sink == order[0]) | (sizes[sink] == 0), 0, jnp.maximum(slack, 0))
    shifted = jax.random.randint(jax.random.fold_in(own, 4), (amount // 2,), 0, 1 << 20) % (slack + 1)
    sizes = sizes.at[source_of].add(-shifted).at[sink].add(shifted)
    members = jnp.searchsorted(jnp.cumsum(sizes), jnp.arange(rows * top), side="right").astype(jnp.int32)
    grid = members.reshape(top, rows).T
    grid = grid[jax.random.permutation(jax.random.fold_in(own, 1), rows)]
    rotation = jax.random.randint(jax.random.fold_in(own, 2), (rows, 1), 0, top)
    return jnp.take_along_axis(grid, (jnp.arange(top)[None, :] + rotation) % top, axis=1)


def portions_of(amount, total, reach, skew, full):
    loads = [(1 << 20) // math.isqrt(grade ** skew) + 1 for grade in range(1, amount + 1)]
    largest = reach if full else min(reach, max(-(-total // amount), total * loads[0] // sum(loads)))
    least = 1 if total - largest >= amount - 1 else 0
    counts, surplus = [largest] + [least] * (amount - 1), total - largest - least * (amount - 1)
    while surplus > 0:
        candidates = [i for i in range(1, amount) if counts[i] < largest] or [i for i in range(1, amount) if counts[i] < reach]
        whole, left = sum([loads[i] for i in candidates]), surplus
        for i in candidates:
            more = min(reach - counts[i], max(1, left * loads[i] // whole), surplus)
            counts[i] = counts[i] + more
            surplus = surplus - more
    return np.array(counts)


def scatter_about(rng, shape, scale, most, cuts=(), held_as=jnp.bfloat16):
    entries = scale * jax.random.normal(rng, shape, jnp.float32)
    if cuts:
        entries = entries * level_of(rng, shape, cuts, -0.22, 0.18)
    return jnp.clip(entries, -most, most).astype(held_as)


def setup_inputs(seed: int = 0, part: int = 0) -> dict:
    seeds = jax.random.split(jax.random.key(seed), 14)
    own_keys = jax.random.split(jax.random.fold_in(seeds[13], part), 14)
    queries = draw_queries(jax.random.fold_in(jax.random.fold_in(seeds[13], part), 71), part)
    latent_cache = draw_latent_cache(jax.random.fold_in(jax.random.fold_in(seeds[13], part), 71), part)
    lengths = draw_lengths(jax.random.fold_in(jax.random.fold_in(seeds[13], part), 71), part)
    assignment = jax.random.permutation(own_keys[3], TOKEN_TOTAL).astype(jnp.int32)
    w_uv = scatter_about(seeds[4], (HEADS, KV_LAT, V_HEAD), KV_LAT ** -0.5, 0.25, ((0, 2),))
    w_o = scatter_about(seeds[5], (HEADS * V_HEAD, D), (4.0 / (HEADS * V_HEAD) ** 0.5), 0.26367188, ((0, 2), (1, 8)))
    residual = scatter_about(own_keys[6], (TOKEN_TOTAL, D), 0.5, 3.0, ((1, 8),))
    gain = jnp.clip(1.0 + 0.18 * jax.random.normal(seeds[7], (D,), jnp.float32), 0.099609375, 1.8984375).astype(jnp.bfloat16)
    expert_ids_keys = jax.random.split(jax.random.fold_in(own_keys[8], 1), TOKEN_TOTAL // TOKEN_TOTAL)
    expert_ids_turns = jax.random.permutation(jax.random.fold_in(own_keys[8], 3), TOKEN_TOTAL // TOKEN_TOTAL)
    expert_ids = jax.vmap(lambda own, number: shared_out(jax.random.fold_in(own_keys[8], 2), own, number, TOKEN_TOTAL, EXPERTS, TOP, CAP, 2))(expert_ids_keys, expert_ids_turns).reshape((TOKEN_TOTAL, TOP))
    expert_weights = draw_expert_weights(jax.random.fold_in(jax.random.fold_in(seeds[13], part), 71), part)
    w_gate = scatter_about(seeds[10], (EXPERTS, D, FF), D ** -0.5, 0.09375, ((0, 16),))
    w_up = scatter_about(seeds[11], (EXPERTS, D, FF), D ** -0.5, 0.09375, ((0, 16),))
    w_down = scatter_about(seeds[12], (EXPERTS, FF, D), FF ** -0.5, 0.1875, ((0, 16),))
    return {"queries": queries, "latent_cache": latent_cache, "lengths": lengths, "assignment": assignment, "w_uv": w_uv, "w_o": w_o, "residual": residual, "gain": gain, "expert_ids": expert_ids, "expert_weights": expert_weights, "w_gate": w_gate, "w_up": w_up, "w_down": w_down}


score_scale = 0.07216878364870323

def reference(queries, latent_cache, lengths, assignment, w_uv, w_o, residual, gain, expert_ids, expert_weights, w_gate, w_up, w_down):
    highest = lax.Precision.HIGHEST

    def attend(packed):
        query_rows, cache_rows, length_one = packed
        cache_wide = cache_rows.astype(jnp.float32)
        score_rows = jnp.dot(query_rows.astype(jnp.float32), cache_wide.T, precision=highest) * score_scale
        in_range = jnp.arange(LMAX, dtype=jnp.int32)[None, :] < length_one
        score_rows = jnp.where(in_range, score_rows, -jnp.inf)
        top_score = lax.optimization_barrier(jnp.max(score_rows, axis=1, keepdims=True))
        weight_rows = jnp.where(in_range, jnp.exp(score_rows - top_score), 0.0)
        weight_sum = lax.optimization_barrier(jnp.sum(weight_rows, axis=1, keepdims=True))
        latent_rows = jnp.dot(weight_rows, cache_wide[:, :KV_LAT], precision=highest) / weight_sum
        return latent_rows.astype(jnp.bfloat16)
    latent_out = lax.map(attend, (queries, latent_cache, lengths))
    head_values = jnp.einsum('thc,hcv->thv', latent_out.astype(jnp.float32), w_uv.astype(jnp.float32), precision=highest)
    head_values = head_values.astype(jnp.bfloat16).reshape(TOKEN_TOTAL, HEADS * V_HEAD)
    request_slot = jnp.zeros((TOKEN_TOTAL,), jnp.int32).at[assignment].set(jnp.arange(TOKEN_TOTAL, dtype=jnp.int32))
    attention = jnp.dot(head_values[request_slot], w_o, preferred_element_type=jnp.float32)
    hidden_state = residual.astype(jnp.float32) + attention
    mean_square = lax.optimization_barrier(jnp.mean(hidden_state * hidden_state, axis=1))
    normed = (hidden_state * lax.rsqrt(mean_square + 1e-06)[:, None] * gain.astype(jnp.float32)).astype(jnp.bfloat16)
    flat_ids = expert_ids.reshape(-1)
    hits = (flat_ids[:, None] == jnp.arange(EXPERTS, dtype=jnp.int32)[None, :]).astype(jnp.int32)
    earlier = jnp.cumsum(hits, axis=0) - hits
    slot_index = lax.optimization_barrier(jnp.sum(earlier * hits, axis=1))
    rows_at = flat_ids * CAP + slot_index
    owners = jnp.repeat(jnp.arange(TOKEN_TOTAL, dtype=jnp.int32), TOP)
    slot_owner = jnp.full((EXPERTS * CAP,), -1, jnp.int32).at[rows_at].set(owners)
    filled = slot_owner >= 0
    expert_rows = jnp.where(filled[:, None], normed[jnp.maximum(slot_owner, 0)], jnp.zeros((), jnp.bfloat16))
    expert_rows = expert_rows.reshape(EXPERTS, CAP, D)

    def apply_expert(packed):
        arrived_rows, gate_weights, up_weights, down_weights = packed
        gate_output = jnp.dot(arrived_rows, gate_weights, preferred_element_type=jnp.float32)
        up_out = jnp.dot(arrived_rows, up_weights, preferred_element_type=jnp.float32)
        hidden_units = (jax.nn.silu(gate_output) * up_out).astype(jnp.bfloat16)
        return jnp.dot(hidden_units, down_weights, preferred_element_type=jnp.float32)
    expert_out = lax.map(apply_expert, (expert_rows, w_gate, w_up, w_down))
    picked = expert_out.reshape(EXPERTS * CAP, D)[rows_at].reshape(TOKEN_TOTAL, TOP, D)
    expert_mix = jnp.einsum('tk,tkd->td', expert_weights, picked, precision=highest)
    return hidden_state + expert_mix
```

```python
import jax
import jax.numpy as jnp
from jax import lax
from jax.experimental import pallas as pl
from jax.experimental.pallas import tpu as pltpu
from jax.sharding import PartitionSpec as P

score_scale = 0.07216878364870323
neg_large = -1e30
MESH = pl.DeviceIdType.MESH


def joined_2(part, axis, combine):
    gathered = jax.tree.map(lambda a: lax.all_gather(a, axis), part)

    def take(source):
        return jax.tree.map(lambda a: lax.dynamic_index_in_dim(a, source, 0, False), gathered)

    return lax.fori_loop(
        1, lax.axis_size(axis), lambda source, state: combine(state, take(source)), take(0)
    )


def softmax_join(first_part, second_part):
    first_max, first_sum, first_acc = first_part
    second_max, second_sum, second_acc = second_part
    joint_max = jnp.maximum(first_max, second_max)
    first_factor = jnp.exp(first_max - joint_max)
    second_factor = jnp.exp(second_max - joint_max)
    joint_sum = first_sum * first_factor + second_sum * second_factor
    joint_acc = first_acc * first_factor[..., None] + second_acc * second_factor[..., None]
    return (joint_max, joint_sum, joint_acc)


def shards(
    queries,
    latent_cache,
    lengths,
    assignment,
    w_uv,
    w_o,
    residual,
    gain,
    expert_ids,
    expert_weights,
    w_gate,
    w_up,
    w_down,
):
    highest = lax.Precision.HIGHEST
    req_rows = queries.shape[0]
    span_len = latent_cache.shape[1]
    lat_width = w_uv.shape[1]
    own_heads = w_uv.shape[0]
    head_group = lax.axis_index(("tensor", "side"))
    position_start = head_group * span_len
    scores = (
        jnp.einsum("rhc,rpc->rhp", queries, latent_cache, preferred_element_type=jnp.float32)
        * score_scale
    )
    places = position_start + lax.broadcasted_iota(jnp.int32, (req_rows, 1, span_len), 2)
    in_range = places < lengths[:, None, None]
    scores = jnp.where(in_range, scores, neg_large)
    top_score = jnp.max(scores, axis=2)
    weight_rows = jnp.where(in_range, jnp.exp(scores - top_score[..., None]), 0.0)
    weight_sum = jnp.sum(weight_rows, axis=2)
    cache_values = latent_cache[:, :, :lat_width].astype(jnp.float32)
    weighted = jnp.einsum("rhp,rpc->rhc", weight_rows, cache_values, precision=highest)
    joined = joined_2((top_score, weight_sum, weighted), ("tensor", "side"), softmax_join)
    head_start = head_group * own_heads
    weight_sum = lax.dynamic_slice_in_dim(joined[1], head_start, own_heads, 1)
    weighted = lax.dynamic_slice_in_dim(joined[2], head_start, own_heads, 1)
    latent_out = (weighted / weight_sum[..., None]).astype(jnp.bfloat16)
    head_values = jnp.einsum(
        "rhc,hcv->rhv", latent_out, w_uv, preferred_element_type=jnp.float32
    ).astype(jnp.bfloat16)
    head_values = head_values.reshape(req_rows, own_heads * w_uv.shape[2])
    slot_terms = jnp.dot(
        lax.all_gather(head_values, "expert", axis=0, tiled=True),
        w_o,
        preferred_element_type=jnp.float32,
    )
    token_count = slot_terms.shape[0]
    request_slot = (
        jnp.zeros((token_count,), jnp.int32)
        .at[assignment]
        .set(jnp.arange(token_count, dtype=jnp.int32))
    )
    attention = lax.psum(slot_terms[request_slot], ("tensor", "side"))
    hidden_state = residual.astype(jnp.float32) + attention
    squares = lax.psum(jnp.sum(hidden_state * hidden_state, axis=1), "expert")
    model_width = w_gate.shape[1]
    normed = (
        hidden_state * lax.rsqrt(squares / model_width + 1e-06)[:, None] * gain.astype(jnp.float32)
    ).astype(jnp.bfloat16)
    top_count = expert_ids.shape[1]
    expert_tally = lax.axis_size("expert")
    side_count = lax.axis_size("side")
    side_index = lax.axis_index("side")
    all_experts = expert_tally * side_count
    capacity = min(token_count, 2 * token_count * top_count // all_experts)
    flat_ids = expert_ids.reshape(-1)
    hits = (flat_ids[:, None] == jnp.arange(all_experts, dtype=jnp.int32)[None, :]).astype(
        jnp.int32
    )
    earlier = jnp.cumsum(hits, axis=0) - hits
    slot_index = jnp.sum(earlier * hits, axis=1)
    own_side = flat_ids % side_count == side_index
    rows_at = jnp.where(
        own_side, flat_ids // side_count * capacity + slot_index, expert_tally * capacity
    )
    owners = jnp.repeat(jnp.arange(token_count, dtype=jnp.int32), top_count)
    slot_owner = (
        jnp.full((expert_tally * capacity,), -1, jnp.int32).at[rows_at].set(owners, mode="drop")
    )
    filled = slot_owner >= 0
    outgoing = jnp.where(
        filled[:, None], normed[jnp.maximum(slot_owner, 0)], jnp.zeros((), jnp.bfloat16)
    )
    outgoing = outgoing.reshape(expert_tally, capacity, normed.shape[1])
    arrived_rows = lax.all_to_all(outgoing, "expert", split_axis=0, concat_axis=2, tiled=True)[0]
    gate_output = jnp.dot(arrived_rows, w_gate[0], preferred_element_type=jnp.float32)
    up_out = jnp.dot(arrived_rows, w_up[0], preferred_element_type=jnp.float32)
    hidden_units = (jax.nn.silu(gate_output) * up_out).astype(jnp.bfloat16)
    partial_rows = jnp.dot(hidden_units, w_down[0], preferred_element_type=jnp.float32)
    summed = lax.psum(partial_rows.astype(jnp.bfloat16), "tensor").astype(jnp.float32)
    sent_back = lax.all_to_all(
        summed[None].astype(jnp.bfloat16), "expert", split_axis=2, concat_axis=0, tiled=True
    ).astype(jnp.float32)
    flat_returned = sent_back.reshape(expert_tally * capacity, sent_back.shape[2])
    picked = flat_returned[jnp.minimum(rows_at, expert_tally * capacity - 1)]
    picked = picked.reshape(token_count, top_count, sent_back.shape[2])
    route_scale = jnp.where(own_side, expert_weights.reshape(-1), 0.0).reshape(
        token_count, top_count
    )
    expert_mix = jnp.einsum("tk,tkd->td", route_scale, picked, precision=highest)
    expert_mix = lax.psum(expert_mix.astype(jnp.bfloat16), "side").astype(jnp.float32)
    return hidden_state + expert_mix


def layer_kernel(
    lengths,
    assignment,
    residual,
    gain,
    expert_ids,
    expert_weights,
    queries_hbm,
    cache_hbm,
    w_uv_hbm,
    w_o_hbm,
    w_gate_hbm,
    w_up_hbm,
    w_down_hbm,
    out,
    queries,
    cache,
    w_uv,
    w_o,
    w_gate,
    w_up,
    w_down,
    own_acc,
    stats_own,
    stats_send,
    stats_recv,
    lat_send,
    lat_recv,
    latent,
    head_wide,
    head_all,
    part_send,
    part_recv,
    hidden,
    scaled_all,
    gate_acc,
    up_acc,
    kept,
    give,
    got,
    mix_send,
    mix_recv,
    last_send,
    last_recv,
    load_sem,
    lat_sems,
    stat_sems,
    head_sems,
    part_sems,
    row_sems,
    got_sems,
    mix_sems,
    last_sems,
):
    f32, bf16 = jnp.float32, jnp.bfloat16
    requests, all_heads, _ = queries.shape
    span = cache.shape[1]
    own_heads, lat_width, v_width = w_uv.shape
    half = own_heads // 2
    tokens, block = residual.shape
    model_width = w_gate.shape[0]
    devices = model_width // block
    chips = devices // 2
    me = lax.axis_index("expert")
    side = lax.axis_index("side")
    core = lax.rem(me, 2)
    chip = lax.div(me, 2)
    sibling = {"expert": chip * 2 + 1 - core}
    across = {"side": 1 - side}

    def chip_at(step):
        return lax.rem(chip + step, chips)

    def on_chip(step):
        return {"expert": chip_at(step) * 2 + core}

    loads = [
        pltpu.make_async_copy(source, target, load_sem.at[i])
        for i, (source, target) in enumerate(
            [
                (queries_hbm, queries),
                (w_uv_hbm, w_uv),
                (w_o_hbm, w_o),
                (w_gate_hbm, w_gate),
                (w_up_hbm, w_up),
                (w_down_hbm, w_down),
            ]
        )
    ]
    cache_loads = [
        pltpu.make_async_copy(cache_hbm.at[r], cache.at[r], load_sem.at[len(loads) + r])
        for r in range(requests)
    ]
    loads[0].start()
    for r in range(requests):
        cache_loads[r].start()
    for load in loads[1:]:
        load.start()

    barrier = pltpu.get_barrier_semaphore()
    partners = [sibling, across] + [on_chip(step) for step in range(1, chips)]
    for partner in partners:
        pl.semaphore_signal(barrier, inc=1, device_id=partner, device_id_type=MESH)
    pl.semaphore_wait(barrier, len(partners))

    def send(source, target, sems, index, where):
        return pltpu.make_async_remote_copy(
            src_ref=source,
            dst_ref=target,
            send_sem=sems.at[0, index],
            recv_sem=sems.at[1, index],
            device_id=where,
            device_id_type=MESH,
        )

    places = side * span + lax.broadcasted_iota(jnp.int32, (all_heads, span), 1)
    lanes = lax.broadcasted_iota(jnp.int32, (all_heads, 128), 1)
    stats = jnp.zeros((all_heads, 128), f32)
    own_rows = pl.ds(pl.multiple_of(side * own_heads, own_heads), own_heads)
    other_rows = pl.ds(pl.multiple_of((1 - side) * own_heads, own_heads), own_heads)
    loads[0].wait()
    lat_copies = []
    for r in range(requests):
        cache_loads[r].wait()
        q = jnp.concatenate([queries[r, own_rows, :], queries[r, other_rows, :]], axis=0)
        scores = lax.dot_general(
            q, cache[r], (((1,), (1,)), ((), ())), preferred_element_type=f32
        )
        in_range = places < lengths[r]
        scores = jnp.where(in_range, scores * score_scale, neg_large)
        top = jnp.max(scores, axis=1, keepdims=True)
        weights = jnp.where(in_range, jnp.exp(scores - top), 0.0)
        total = jnp.sum(weights, axis=1, keepdims=True)
        high = weights.astype(bf16)
        low = (weights - high.astype(f32)).astype(bf16)
        acc = jnp.dot(
            jnp.concatenate([high, low], axis=0),
            cache[r, :, :lat_width],
            preferred_element_type=f32,
        )
        acc = acc[:all_heads] + acc[all_heads:]
        stats = jnp.where(lanes == 2 * r, top, jnp.where(lanes == 2 * r + 1, total, stats))
        own_acc[r] = acc[:own_heads]
        other_total = total[own_heads:]
        lat_send[r] = jnp.where(
            other_total > 0.0, acc[own_heads:] / jnp.maximum(other_total, 1e-30), 0.0
        ).astype(bf16)
        copy = send(lat_send.at[r], lat_recv.at[r], lat_sems, r, across)
        copy.start()
        lat_copies.append(copy)
    stats_own[...] = stats[:own_heads]
    stats_send[...] = stats[own_heads:]
    stat_copy = send(stats_send, stats_recv, stat_sems, 0, across)
    stat_copy.start()

    stat_copy.wait_recv()
    first = stats_own[...]
    second = stats_recv[...]
    for r in range(requests):
        first_top, first_sum = first[:, 2 * r : 2 * r + 1], first[:, 2 * r + 1 : 2 * r + 2]
        second_top, second_sum = second[:, 2 * r : 2 * r + 1], second[:, 2 * r + 1 : 2 * r + 2]
        joint = jnp.maximum(first_top, second_top)
        first_factor = jnp.exp(first_top - joint)
        second_factor = jnp.exp(second_top - joint) * second_sum
        inverse = 1.0 / (first_sum * first_factor + second_factor)
        lat_copies[r].wait_recv()
        latent[r] = own_acc[r] * (first_factor * inverse) + lat_recv[r].astype(f32) * (
            second_factor * inverse
        )

    loads[1].wait()
    for h in range(own_heads):
        rows = latent[:, h, :].astype(bf16)
        head_wide[
            (h // half) * requests : (h // half + 1) * requests,
            (h % half) * v_width : (h % half + 1) * v_width,
        ] = jnp.dot(rows, w_uv[h], preferred_element_type=f32)
    pair_rows = 2 * requests

    def head_slot(device):
        return head_all.at[pl.ds(pl.multiple_of(device * pair_rows, pair_rows), pair_rows), :]

    def row_slot(device):
        return scaled_all.at[pl.ds(pl.multiple_of(device * tokens, tokens), tokens), :]

    def gather(slot, sems):
        far = [
            send(slot(me), slot(me), sems, step - 1, on_chip(step)) for step in range(1, chips)
        ]
        near = [send(slot(me), slot(me), sems, chips - 1, sibling)]
        for copy in far + near:
            copy.start()
        for step in range(1, chips):
            near.append(
                send(
                    slot(chip_at(chips - step) * 2 + core),
                    slot(chip_at(chips - step) * 2 + core),
                    sems,
                    chips - 1 + step,
                    sibling,
                )
            )
        return far, near

    head_slot(me)[...] = head_wide[...].astype(bf16)
    far, near = gather(head_slot, head_sems)
    for step in range(1, chips):
        far[step - 1].wait_recv()
        near[step].start()
    for step in range(chips):
        near[step].wait_recv()
    head_copies = far + near
    loads[2].wait()
    depth = half * v_width
    first_term = jnp.dot(head_all[...], w_o[:depth, :], preferred_element_type=f32)
    second_term = jnp.dot(head_all[...], w_o[depth:, :], preferred_element_type=f32)
    slot_terms = (
        first_term.reshape(devices, 2, requests, block)[:, 0]
        + second_term.reshape(devices, 2, requests, block)[:, 1]
    ).reshape(tokens, block)
    order = (
        lax.broadcasted_iota(jnp.int32, (tokens, tokens), 0) == assignment[...]
    ).astype(f32).astype(bf16)
    part_send[...] = jnp.dot(
        order, slot_terms.astype(bf16), preferred_element_type=f32
    ).astype(bf16)
    part_copy = send(part_send, part_recv, part_sems, 0, across)
    part_copy.start()
    base = residual[...].astype(f32)
    scale = gain[...].astype(f32)
    part_copy.wait_recv()
    state = base + (part_send[...].astype(f32) + part_recv[...].astype(f32))
    hidden[...] = state
    squares = jnp.sum(state * state, axis=1, keepdims=True)
    sq_high = squares.astype(bf16).astype(f32)
    sq_mid = (squares - sq_high).astype(bf16).astype(f32)
    sq_low = squares - sq_high - sq_mid
    extra = scaled_all.shape[1] - block
    extra_lanes = lax.broadcasted_iota(jnp.int32, (tokens, extra), 1)
    tail = jnp.where(
        extra_lanes == 0,
        sq_high,
        jnp.where(extra_lanes == 1, sq_mid, jnp.where(extra_lanes == 2, sq_low, 0.0)),
    )
    row_slot(me)[...] = jnp.concatenate([state * scale, tail], axis=1).astype(bf16)
    far, near = gather(row_slot, row_sems)
    row_copies = far + near

    loads[3].wait()
    loads[4].wait()
    square_sum = jnp.zeros((tokens, 1), f32)

    def absorb(device, begin, square_sum):
        rows = row_slot(device)[...]
        part = rows[:, :block]
        weight_rows = pl.ds(pl.multiple_of(device * block, 64), block)
        gate_part = jnp.dot(part, w_gate[weight_rows, :], preferred_element_type=f32)
        up_part = jnp.dot(part, w_up[weight_rows, :], preferred_element_type=f32)
        if begin:
            gate_acc[...] = gate_part
            up_acc[...] = up_part
        else:
            gate_acc[...] += gate_part
            up_acc[...] += up_part
        return square_sum + jnp.sum(rows[:, block:].astype(f32), axis=1, keepdims=True)

    square_sum = absorb(me, True, square_sum)
    near[0].wait_recv()
    square_sum = absorb(chip * 2 + 1 - core, False, square_sum)
    for step in (1, 3, 2) if chips == 4 else range(1, chips):
        far[step - 1].wait_recv()
        near[step].start()
        square_sum = absorb(chip_at(chips - step) * 2 + core, False, square_sum)
        near[step].wait_recv()
        square_sum = absorb(chip_at(chips - step) * 2 + 1 - core, False, square_sum)
    norm = lax.rsqrt(square_sum / model_width + 1e-06)
    gate_output = gate_acc[...] * norm
    units = (gate_output * jax.nn.sigmoid(gate_output) * (up_acc[...] * norm)).astype(bf16)

    expert = me * 2 + side
    route = jnp.sum(
        jnp.where(expert_ids[...] == expert, expert_weights[...], 0.0), axis=1, keepdims=True
    )
    loads[5].wait()
    got_copies, mix_copies = [], []

    def forward(step):
        got_copies[step].wait_recv()
        both = kept[step] + got[step].astype(f32)
        if step == chips - 1:
            return both
        mix_send[step] = both.astype(bf16)
        copy = send(mix_send.at[step], mix_recv.at[step], mix_sems, step, on_chip(step + 1))
        copy.start()
        mix_copies.append(copy)

    for step in range(chips):
        columns = pl.ds(pl.multiple_of(chip_at(step + 1) * (2 * block), 128), 2 * block)
        result = jnp.dot(units, w_down[:, columns], preferred_element_type=f32) * route
        left, right = result[:, :block], result[:, block:]
        kept[step] = jnp.where(core == 0, left, right)
        give[step] = jnp.where(core == 0, right, left).astype(bf16)
        copy = send(give.at[step], got.at[step], got_sems, step, sibling)
        copy.start()
        got_copies.append(copy)
        if step:
            forward(step - 1)
    mixed = forward(chips - 1)
    for step in range(chips - 1):
        mix_copies[step].wait_recv()
        mixed = mixed + mix_recv[step].astype(f32)
    last_send[...] = mixed.astype(bf16)
    last_copy = send(last_send, last_recv, last_sems, 0, across)
    last_copy.start()
    last_copy.wait_recv()
    out[...] = hidden[...] + (last_send[...].astype(f32) + last_recv[...].astype(f32))
    for copy in (
        lat_copies + [stat_copy] + head_copies + [part_copy] + row_copies + got_copies
        + mix_copies + [last_copy]
    ):
        copy.wait_send()


def fused(
    queries,
    latent_cache,
    lengths,
    assignment,
    w_uv,
    w_o,
    residual,
    gain,
    expert_ids,
    expert_weights,
    w_gate,
    w_up,
    w_down,
):
    f32, bf16 = jnp.float32, jnp.bfloat16
    requests = queries.shape[0]
    own_heads, lat_width, v_width = w_uv.shape
    tokens, block = residual.shape
    model_width, units = w_gate.shape[1:]
    chips = model_width // block // 2
    wide = -(-(block + 3) // 128) * 128
    vmem = pl.BlockSpec(memory_space=pltpu.VMEM)
    hbm = pl.BlockSpec(memory_space=pl.ANY)
    buffer = pltpu.VMEM
    pairs = pltpu.SemaphoreType.DMA
    return pl.pallas_call(
        layer_kernel,
        out_shape=jax.ShapeDtypeStruct((tokens, block), f32),
        in_specs=[pl.BlockSpec(memory_space=pltpu.SMEM)] + [vmem] * 5 + [hbm] * 7,
        out_specs=vmem,
        scratch_shapes=[
            buffer(queries.shape, bf16),
            buffer(latent_cache.shape, bf16),
            buffer(w_uv.shape, bf16),
            buffer(w_o.shape, bf16),
            buffer((model_width, units), bf16),
            buffer((model_width, units), bf16),
            buffer((units, model_width), bf16),
            buffer((requests, own_heads, lat_width), f32),
            buffer((own_heads, 128), f32),
            buffer((own_heads, 128), f32),
            buffer((own_heads, 128), f32),
            buffer((requests, own_heads, lat_width), bf16),
            buffer((requests, own_heads, lat_width), bf16),
            buffer((requests, own_heads, lat_width), f32),
            buffer((2 * requests, own_heads * v_width // 2), f32),
            buffer((2 * tokens, own_heads * v_width // 2), bf16),
            buffer((tokens, block), bf16),
            buffer((tokens, block), bf16),
            buffer((tokens, block), f32),
            buffer((2 * chips * tokens, wide), bf16),
            buffer((tokens, units), f32),
            buffer((tokens, units), f32),
            buffer((chips, tokens, block), f32),
            buffer((chips, tokens, block), bf16),
            buffer((chips, tokens, block), bf16),
            buffer((chips - 1, tokens, block), bf16),
            buffer((chips - 1, tokens, block), bf16),
            buffer((tokens, block), bf16),
            buffer((tokens, block), bf16),
            pairs((6 + requests,)),
            pairs((2, requests)),
            pairs((2, 1)),
            pairs((2, 2 * chips - 1)),
            pairs((2, 1)),
            pairs((2, 2 * chips - 1)),
            pairs((2, chips)),
            pairs((2, chips - 1)),
            pairs((2, 1)),
        ],
        compiler_params=pltpu.CompilerParams(
            collective_id=0, has_side_effects=True, vmem_limit_bytes=58 * 1024 * 1024
        ),
    )(
        lengths,
        assignment[None, :],
        residual,
        gain[None, :],
        expert_ids,
        expert_weights,
        queries,
        latent_cache,
        w_uv,
        w_o,
        w_gate[0],
        w_up[0],
        w_down[0],
    )


def solution(mesh):
    in_specs = (
        P(("groups", "expert"), None, None),
        P(("groups", "expert"), ("tensor", "side"), None),
        P(("groups", "expert")),
        P("groups"),
        P(("tensor", "side"), None, None),
        P(("tensor", "side"), "expert"),
        P("groups", "expert"),
        P("expert"),
        P("groups", None),
        P("groups", None),
        P(("expert", "side"), None, "tensor"),
        P(("expert", "side"), None, "tensor"),
        P(("expert", "side"), "tensor", None),
    )
    out_specs = P("groups", "expert")
    sizes = mesh.shape
    one_kernel = sizes["tensor"] == 1 and sizes["side"] == 2 and sizes["expert"] == 8
    body = fused if one_kernel else shards
    return jax.shard_map(body, mesh=mesh, in_specs=in_specs, out_specs=out_specs, check_vma=False)
```

```python
import jax
import jax.numpy as jnp
from jax import lax
from jax.experimental import pallas as pl
from jax.experimental.pallas import tpu as pltpu
from jax.sharding import PartitionSpec as P

score_scale = 0.07216878364870323
neg_large = -1e30
MESH = pl.DeviceIdType.MESH


def joined_2(part, axis, combine):
    gathered = jax.tree.map(lambda a: lax.all_gather(a, axis), part)

    def take(source):
        return jax.tree.map(lambda a: lax.dynamic_index_in_dim(a, source, 0, False), gathered)

    return lax.fori_loop(
        1, lax.axis_size(axis), lambda source, state: combine(state, take(source)), take(0)
    )


def softmax_join(first_part, second_part):
    first_max, first_sum, first_acc = first_part
    second_max, second_sum, second_acc = second_part
    joint_max = jnp.maximum(first_max, second_max)
    first_factor = jnp.exp(first_max - joint_max)
    second_factor = jnp.exp(second_max - joint_max)
    joint_sum = first_sum * first_factor + second_sum * second_factor
    joint_acc = first_acc * first_factor[..., None] + second_acc * second_factor[..., None]
    return (joint_max, joint_sum, joint_acc)


def shards(
    queries,
    latent_cache,
    lengths,
    assignment,
    w_uv,
    w_o,
    residual,
    gain,
    expert_ids,
    expert_weights,
    w_gate,
    w_up,
    w_down,
):
    highest = lax.Precision.HIGHEST
    req_rows = queries.shape[0]
    span_len = latent_cache.shape[1]
    lat_width = w_uv.shape[1]
    own_heads = w_uv.shape[0]
    head_group = lax.axis_index(("tensor", "side"))
    position_start = head_group * span_len
    scores = (
        jnp.einsum("rhc,rpc->rhp", queries, latent_cache, preferred_element_type=jnp.float32)
        * score_scale
    )
    places = position_start + lax.broadcasted_iota(jnp.int32, (req_rows, 1, span_len), 2)
    in_range = places < lengths[:, None, None]
    scores = jnp.where(in_range, scores, neg_large)
    top_score = jnp.max(scores, axis=2)
    weight_rows = jnp.where(in_range, jnp.exp(scores - top_score[..., None]), 0.0)
    weight_sum = jnp.sum(weight_rows, axis=2)
    cache_values = latent_cache[:, :, :lat_width].astype(jnp.float32)
    weighted = jnp.einsum("rhp,rpc->rhc", weight_rows, cache_values, precision=highest)
    joined = joined_2((top_score, weight_sum, weighted), ("tensor", "side"), softmax_join)
    head_start = head_group * own_heads
    weight_sum = lax.dynamic_slice_in_dim(joined[1], head_start, own_heads, 1)
    weighted = lax.dynamic_slice_in_dim(joined[2], head_start, own_heads, 1)
    latent_out = (weighted / weight_sum[..., None]).astype(jnp.bfloat16)
    head_values = jnp.einsum(
        "rhc,hcv->rhv", latent_out, w_uv, preferred_element_type=jnp.float32
    ).astype(jnp.bfloat16)
    head_values = head_values.reshape(req_rows, own_heads * w_uv.shape[2])
    slot_terms = jnp.dot(
        lax.all_gather(head_values, "expert", axis=0, tiled=True),
        w_o,
        preferred_element_type=jnp.float32,
    )
    token_count = slot_terms.shape[0]
    request_slot = (
        jnp.zeros((token_count,), jnp.int32)
        .at[assignment]
        .set(jnp.arange(token_count, dtype=jnp.int32))
    )
    attention = lax.psum(slot_terms[request_slot], ("tensor", "side"))
    hidden_state = residual.astype(jnp.float32) + attention
    squares = lax.psum(jnp.sum(hidden_state * hidden_state, axis=1), "expert")
    model_width = w_gate.shape[1]
    normed = (
        hidden_state * lax.rsqrt(squares / model_width + 1e-06)[:, None] * gain.astype(jnp.float32)
    ).astype(jnp.bfloat16)
    top_count = expert_ids.shape[1]
    expert_tally = lax.axis_size("expert")
    side_count = lax.axis_size("side")
    side_index = lax.axis_index("side")
    all_experts = expert_tally * side_count
    capacity = min(token_count, 2 * token_count * top_count // all_experts)
    flat_ids = expert_ids.reshape(-1)
    hits = (flat_ids[:, None] == jnp.arange(all_experts, dtype=jnp.int32)[None, :]).astype(
        jnp.int32
    )
    earlier = jnp.cumsum(hits, axis=0) - hits
    slot_index = jnp.sum(earlier * hits, axis=1)
    own_side = flat_ids % side_count == side_index
    rows_at = jnp.where(
        own_side, flat_ids // side_count * capacity + slot_index, expert_tally * capacity
    )
    owners = jnp.repeat(jnp.arange(token_count, dtype=jnp.int32), top_count)
    slot_owner = (
        jnp.full((expert_tally * capacity,), -1, jnp.int32).at[rows_at].set(owners, mode="drop")
    )
    filled = slot_owner >= 0
    outgoing = jnp.where(
        filled[:, None], normed[jnp.maximum(slot_owner, 0)], jnp.zeros((), jnp.bfloat16)
    )
    outgoing = outgoing.reshape(expert_tally, capacity, normed.shape[1])
    arrived_rows = lax.all_to_all(outgoing, "expert", split_axis=0, concat_axis=2, tiled=True)[0]
    gate_output = jnp.dot(arrived_rows, w_gate[0], preferred_element_type=jnp.float32)
    up_out = jnp.dot(arrived_rows, w_up[0], preferred_element_type=jnp.float32)
    hidden_units = (jax.nn.silu(gate_output) * up_out).astype(jnp.bfloat16)
    partial_rows = jnp.dot(hidden_units, w_down[0], preferred_element_type=jnp.float32)
    summed = lax.psum(partial_rows.astype(jnp.bfloat16), "tensor").astype(jnp.float32)
    sent_back = lax.all_to_all(
        summed[None].astype(jnp.bfloat16), "expert", split_axis=2, concat_axis=0, tiled=True
    ).astype(jnp.float32)
    flat_returned = sent_back.reshape(expert_tally * capacity, sent_back.shape[2])
    picked = flat_returned[jnp.minimum(rows_at, expert_tally * capacity - 1)]
    picked = picked.reshape(token_count, top_count, sent_back.shape[2])
    route_scale = jnp.where(own_side, expert_weights.reshape(-1), 0.0).reshape(
        token_count, top_count
    )
    expert_mix = jnp.einsum("tk,tkd->td", route_scale, picked, precision=highest)
    expert_mix = lax.psum(expert_mix.astype(jnp.bfloat16), "side").astype(jnp.float32)
    return hidden_state + expert_mix


def layer_kernel(
    lengths,
    assignment,
    residual,
    gain,
    expert_ids,
    expert_weights,
    queries_hbm,
    cache_hbm,
    w_uv_hbm,
    w_o_hbm,
    w_gate_hbm,
    w_up_hbm,
    w_down_hbm,
    out,
    queries,
    cache,
    w_uv,
    w_o,
    w_gate,
    w_up,
    w_down,
    own_acc,
    stats_own,
    stats_send,
    stats_recv,
    lat_send,
    lat_recv,
    latent,
    head_wide,
    head_all,
    part_send,
    part_recv,
    hidden,
    scaled_all,
    gate_acc,
    up_acc,
    kept,
    give,
    got,
    mix_send,
    mix_recv,
    last_send,
    last_recv,
    load_sem,
    lat_sems,
    stat_sems,
    head_sems,
    part_sems,
    row_sems,
    got_sems,
    mix_sems,
    last_sems,
):
    f32, bf16 = jnp.float32, jnp.bfloat16
    requests, all_heads, _ = queries.shape
    span = cache.shape[2]
    own_heads, lat_width, v_width = w_uv.shape
    half = own_heads // 2
    tokens, block = residual.shape
    model_width = w_gate.shape[0]
    devices = model_width // block
    chips = devices // 2
    me = lax.axis_index("expert")
    side = lax.axis_index("side")
    core = lax.rem(me, 2)
    chip = lax.div(me, 2)
    sibling = {"expert": chip * 2 + 1 - core}
    across = {"side": 1 - side}

    def dot_turned(left, right):
        return lax.dot_general(
            left, right, (((1,), (1,)), ((), ())), preferred_element_type=f32
        )

    def chip_at(step):
        return lax.rem(chip + step, chips)

    def on_chip(step):
        return {"expert": chip_at(step) * 2 + core}

    loads = [
        pltpu.make_async_copy(source, target, load_sem.at[i])
        for i, (source, target) in enumerate(
            [
                (queries_hbm, queries),
                (w_uv_hbm, w_uv),
                (w_o_hbm, w_o),
                (w_gate_hbm, w_gate),
                (w_up_hbm, w_up),
                (w_down_hbm, w_down),
            ]
        )
    ]
    cache_loads = [
        pltpu.make_async_copy(cache_hbm.at[r], cache.at[r], load_sem.at[len(loads) + r])
        for r in range(requests)
    ]
    loads[0].start()
    for r in range(requests):
        cache_loads[r].start()
    for load in loads[1:]:
        load.start()

    barrier = pltpu.get_barrier_semaphore()
    partners = [sibling, across] + [on_chip(step) for step in range(1, chips)]
    for partner in partners:
        pl.semaphore_signal(barrier, inc=1, device_id=partner, device_id_type=MESH)
    pl.semaphore_wait(barrier, len(partners))

    def send(source, target, sems, index, where):
        return pltpu.make_async_remote_copy(
            src_ref=source,
            dst_ref=target,
            send_sem=sems.at[0, index],
            recv_sem=sems.at[1, index],
            device_id=where,
            device_id_type=MESH,
        )

    places = side * span + lax.broadcasted_iota(jnp.int32, (all_heads, span), 1)
    lanes = lax.broadcasted_iota(jnp.int32, (all_heads, 128), 1)
    stats = jnp.zeros((all_heads, 128), f32)
    own_rows = pl.ds(pl.multiple_of(side * own_heads, own_heads), own_heads)
    other_rows = pl.ds(pl.multiple_of((1 - side) * own_heads, own_heads), own_heads)
    loads[0].wait()
    lat_copies = []
    for r in range(requests):
        cache_loads[r].wait()
        q = jnp.concatenate([queries[r, own_rows, :], queries[r, other_rows, :]], axis=0)
        scores = jnp.dot(q, cache[r], preferred_element_type=f32)
        in_range = places < lengths[r]
        scores = jnp.where(in_range, scores * score_scale, neg_large)
        top = jnp.max(scores, axis=1, keepdims=True)
        weights = jnp.where(in_range, jnp.exp(scores - top), 0.0)
        total = jnp.sum(weights, axis=1, keepdims=True)
        high = weights.astype(bf16)
        low = (weights - high.astype(f32)).astype(bf16)
        acc = dot_turned(jnp.concatenate([high, low], axis=0), cache[r, :lat_width, :])
        acc = acc[:all_heads] + acc[all_heads:]
        stats = jnp.where(lanes == 2 * r, top, jnp.where(lanes == 2 * r + 1, total, stats))
        own_acc[r] = acc[:own_heads]
        other_total = total[own_heads:]
        lat_send[r] = jnp.where(
            other_total > 0.0, acc[own_heads:] / jnp.maximum(other_total, 1e-30), 0.0
        ).astype(bf16)
        copy = send(lat_send.at[r], lat_recv.at[r], lat_sems, r, across)
        copy.start()
        lat_copies.append(copy)
    stats_own[...] = stats[:own_heads]
    stats_send[...] = stats[own_heads:]
    stat_copy = send(stats_send, stats_recv, stat_sems, 0, across)
    stat_copy.start()

    stat_copy.wait_recv()
    first = stats_own[...]
    second = stats_recv[...]
    for r in range(requests):
        first_top, first_sum = first[:, 2 * r : 2 * r + 1], first[:, 2 * r + 1 : 2 * r + 2]
        second_top, second_sum = second[:, 2 * r : 2 * r + 1], second[:, 2 * r + 1 : 2 * r + 2]
        joint = jnp.maximum(first_top, second_top)
        first_factor = jnp.exp(first_top - joint)
        second_factor = jnp.exp(second_top - joint) * second_sum
        inverse = 1.0 / (first_sum * first_factor + second_factor)
        lat_copies[r].wait_recv()
        latent[r] = own_acc[r] * (first_factor * inverse) + lat_recv[r].astype(f32) * (
            second_factor * inverse
        )

    loads[1].wait()
    for h in range(own_heads):
        rows = latent[:, h, :].astype(bf16)
        head_wide[
            (h // half) * requests : (h // half + 1) * requests,
            (h % half) * v_width : (h % half + 1) * v_width,
        ] = jnp.dot(rows, w_uv[h], preferred_element_type=f32)
    pair_rows = 2 * requests

    def head_slot(device):
        return head_all.at[pl.ds(pl.multiple_of(device * pair_rows, pair_rows), pair_rows), :]

    def row_slot(device):
        return scaled_all.at[pl.ds(pl.multiple_of(device * tokens, tokens), tokens), :]

    def gather(slot, sems):
        far = [
            send(slot(me), slot(me), sems, step - 1, on_chip(step)) for step in range(1, chips)
        ]
        near = [send(slot(me), slot(me), sems, chips - 1, sibling)]
        for copy in far + near:
            copy.start()
        for step in range(1, chips):
            near.append(
                send(
                    slot(chip_at(chips - step) * 2 + core),
                    slot(chip_at(chips - step) * 2 + core),
                    sems,
                    chips - 1 + step,
                    sibling,
                )
            )
        return far, near

    head_slot(me)[...] = head_wide[...].astype(bf16)
    far, near = gather(head_slot, head_sems)
    for step in range(1, chips):
        far[step - 1].wait_recv()
        near[step].start()
    for step in range(chips):
        near[step].wait_recv()
    head_copies = far + near
    loads[2].wait()
    depth = half * v_width
    first_term = dot_turned(head_all[...], w_o[:, :depth])
    second_term = dot_turned(head_all[...], w_o[:, depth:])
    slot_terms = (
        first_term.reshape(devices, 2, requests, block)[:, 0]
        + second_term.reshape(devices, 2, requests, block)[:, 1]
    ).reshape(tokens, block)
    order = (
        lax.broadcasted_iota(jnp.int32, (tokens, tokens), 0) == assignment[...]
    ).astype(f32).astype(bf16)
    part_send[...] = jnp.dot(
        order, slot_terms.astype(bf16), preferred_element_type=f32
    ).astype(bf16)
    part_copy = send(part_send, part_recv, part_sems, 0, across)
    part_copy.start()
    base = residual[...].astype(f32)
    scale = gain[...].astype(f32)[None, :]
    part_copy.wait_recv()
    state = base + (part_send[...].astype(f32) + part_recv[...].astype(f32))
    hidden[...] = state
    squares = jnp.sum(state * state, axis=1, keepdims=True)
    sq_high = squares.astype(bf16).astype(f32)
    sq_mid = (squares - sq_high).astype(bf16).astype(f32)
    sq_low = squares - sq_high - sq_mid
    extra = scaled_all.shape[1] - block
    extra_lanes = lax.broadcasted_iota(jnp.int32, (tokens, extra), 1)
    tail = jnp.where(
        extra_lanes == 0,
        sq_high,
        jnp.where(extra_lanes == 1, sq_mid, jnp.where(extra_lanes == 2, sq_low, 0.0)),
    )
    row_slot(me)[...] = jnp.concatenate([state * scale, tail], axis=1).astype(bf16)
    far, near = gather(row_slot, row_sems)
    row_copies = far + near

    loads[3].wait()
    loads[4].wait()
    square_sum = jnp.zeros((tokens, 1), f32)

    def absorb(device, begin, square_sum):
        rows = row_slot(device)[...]
        part = rows[:, :block]
        weight_rows = pl.ds(pl.multiple_of(device * block, 64), block)
        gate_part = jnp.dot(part, w_gate[weight_rows, :], preferred_element_type=f32)
        up_part = jnp.dot(part, w_up[weight_rows, :], preferred_element_type=f32)
        if begin:
            gate_acc[...] = gate_part
            up_acc[...] = up_part
        else:
            gate_acc[...] += gate_part
            up_acc[...] += up_part
        return square_sum + jnp.sum(rows[:, block:].astype(f32), axis=1, keepdims=True)

    square_sum = absorb(me, True, square_sum)
    near[0].wait_recv()
    square_sum = absorb(chip * 2 + 1 - core, False, square_sum)
    for step in (1, 3, 2) if chips == 4 else range(1, chips):
        far[step - 1].wait_recv()
        near[step].start()
        square_sum = absorb(chip_at(chips - step) * 2 + core, False, square_sum)
        near[step].wait_recv()
        square_sum = absorb(chip_at(chips - step) * 2 + 1 - core, False, square_sum)
    norm = lax.rsqrt(square_sum / model_width + 1e-06)
    gate_output = gate_acc[...] * norm
    units = (gate_output * jax.nn.sigmoid(gate_output) * (up_acc[...] * norm)).astype(bf16)

    expert = me * 2 + side
    route_row = jnp.sum(
        jnp.where(expert_ids[...] == expert, expert_weights[...], 0.0), axis=0, keepdims=True
    )
    diagonal = lax.broadcasted_iota(jnp.int32, (tokens, tokens), 0) == lax.broadcasted_iota(
        jnp.int32, (tokens, tokens), 1
    )
    route = jnp.sum(jnp.where(diagonal, route_row, 0.0), axis=1, keepdims=True)
    loads[5].wait()
    got_copies, mix_copies = [], []

    def forward(step):
        got_copies[step].wait_recv()
        both = kept[step] + got[step].astype(f32)
        if step == chips - 1:
            return both
        mix_send[step] = both.astype(bf16)
        copy = send(mix_send.at[step], mix_recv.at[step], mix_sems, step, on_chip(step + 1))
        copy.start()
        mix_copies.append(copy)

    for step in range(chips):
        columns = pl.ds(pl.multiple_of(chip_at(step + 1) * (2 * block), 128), 2 * block)
        result = jnp.dot(units, w_down[:, columns], preferred_element_type=f32) * route
        left, right = result[:, :block], result[:, block:]
        kept[step] = jnp.where(core == 0, left, right)
        give[step] = jnp.where(core == 0, right, left).astype(bf16)
        copy = send(give.at[step], got.at[step], got_sems, step, sibling)
        copy.start()
        got_copies.append(copy)
        if step:
            forward(step - 1)
    mixed = forward(chips - 1)
    for step in range(chips - 1):
        mix_copies[step].wait_recv()
        mixed = mixed + mix_recv[step].astype(f32)
    last_send[...] = mixed.astype(bf16)
    last_copy = send(last_send, last_recv, last_sems, 0, across)
    last_copy.start()
    last_copy.wait_recv()
    out[...] = hidden[...] + (last_send[...].astype(f32) + last_recv[...].astype(f32))
    for copy in (
        lat_copies + [stat_copy] + head_copies + [part_copy] + row_copies + got_copies
        + mix_copies + [last_copy]
    ):
        copy.wait_send()


def fused(
    queries,
    latent_cache,
    lengths,
    assignment,
    w_uv,
    w_o,
    residual,
    gain,
    expert_ids,
    expert_weights,
    w_gate,
    w_up,
    w_down,
):
    f32, bf16 = jnp.float32, jnp.bfloat16
    requests = queries.shape[0]
    own_heads, lat_width, v_width = w_uv.shape
    tokens, block = residual.shape
    model_width, units = w_gate.shape[1:]
    chips = model_width // block // 2
    wide = -(-(block + 3) // 128) * 128
    vmem = pl.BlockSpec(memory_space=pltpu.VMEM)
    hbm = pl.BlockSpec(memory_space=pl.ANY)
    buffer = pltpu.VMEM
    pairs = pltpu.SemaphoreType.DMA
    return pl.pallas_call(
        layer_kernel,
        out_shape=jax.ShapeDtypeStruct((tokens, block), f32),
        in_specs=[pl.BlockSpec(memory_space=pltpu.SMEM)] + [vmem] * 5 + [hbm] * 7,
        out_specs=vmem,
        scratch_shapes=[
            buffer(queries.shape, bf16),
            buffer((requests, latent_cache.shape[2], latent_cache.shape[1]), bf16),
            buffer(w_uv.shape, bf16),
            buffer(w_o.shape[::-1], bf16),
            buffer((model_width, units), bf16),
            buffer((model_width, units), bf16),
            buffer((units, model_width), bf16),
            buffer((requests, own_heads, lat_width), f32),
            buffer((own_heads, 128), f32),
            buffer((own_heads, 128), f32),
            buffer((own_heads, 128), f32),
            buffer((requests, own_heads, lat_width), bf16),
            buffer((requests, own_heads, lat_width), bf16),
            buffer((requests, own_heads, lat_width), f32),
            buffer((2 * requests, own_heads * v_width // 2), f32),
            buffer((2 * tokens, own_heads * v_width // 2), bf16),
            buffer((tokens, block), bf16),
            buffer((tokens, block), bf16),
            buffer((tokens, block), f32),
            buffer((2 * chips * tokens, wide), bf16),
            buffer((tokens, units), f32),
            buffer((tokens, units), f32),
            buffer((chips, tokens, block), f32),
            buffer((chips, tokens, block), bf16),
            buffer((chips, tokens, block), bf16),
            buffer((chips - 1, tokens, block), bf16),
            buffer((chips - 1, tokens, block), bf16),
            buffer((tokens, block), bf16),
            buffer((tokens, block), bf16),
            pairs((6 + requests,)),
            pairs((2, requests)),
            pairs((2, 1)),
            pairs((2, 2 * chips - 1)),
            pairs((2, 1)),
            pairs((2, 2 * chips - 1)),
            pairs((2, chips)),
            pairs((2, chips - 1)),
            pairs((2, 1)),
        ],
        compiler_params=pltpu.CompilerParams(
            collective_id=0, has_side_effects=True, vmem_limit_bytes=58 * 1024 * 1024
        ),
    )(
        lengths,
        assignment[None, :],
        residual,
        gain,
        expert_ids.T,
        expert_weights.T,
        queries,
        latent_cache.transpose(0, 2, 1),
        w_uv,
        w_o.T,
        w_gate[0],
        w_up[0],
        w_down[0],
    )


def solution(mesh):
    in_specs = (
        P(("groups", "expert"), None, None),
        P(("groups", "expert"), ("tensor", "side"), None),
        P(("groups", "expert")),
        P("groups"),
        P(("tensor", "side"), None, None),
        P(("tensor", "side"), "expert"),
        P("groups", "expert"),
        P("expert"),
        P("groups", None),
        P("groups", None),
        P(("expert", "side"), None, "tensor"),
        P(("expert", "side"), None, "tensor"),
        P(("expert", "side"), "tensor", None),
    )
    out_specs = P("groups", "expert")
    sizes = mesh.shape
    one_kernel = sizes["tensor"] == 1 and sizes["side"] == 2 and sizes["expert"] == 8
    body = fused if one_kernel else shards
    return jax.shard_map(body, mesh=mesh, in_specs=in_specs, out_specs=out_specs, check_vma=False)
```
